32 devices in a mesh: row: 4 (over z), col: 4 (over y, x), pair: 2 (over core).
Axes of the slice: x: 2, y: 2, z: 4, core: 2. Of those that a mesh axis runs over, the one named last changes fastest.
Arguments:
- integrals: bfloat16 [2048, 2048], P('row', ('col', 'pair')), may hold values from -0.1875 to 0.1875
- int_mask: int32 [32, 32], P('row', ('col', 'pair')), may hold values 0 or 1
- amplitudes: bfloat16 [2048, 2048], P('row', ('col', 'pair')), may hold values from -6 to 6
- domain_mask: int32 [32, 2048], P('row', ('col', 'pair')), may hold values 0 or 1
- virt_energy: float32 [2048], P('row'), may hold values from 0.5 to 4
- occ_energy: float32 [2048], P(('col', 'pair')), may hold values from -3 to -0.5
Outputs:
- update: float32 [2048, 2048], P('row', ('col', 'pair'))
The draws below stay inside these ranges and needn't reach their ends.
All inputs are finite; a program needn't handle non-finite values. No bound on the sum of `int_mask` or of `domain_mask` on one device may be relied on, other than what follows from the above.
Results may differ from the reference program's by a relative error of at most 0.0003.
Values may be sent and summed in bfloat16 or wider, within the bound.
A program may use at most 64 MiB of HBM per device.

```python
import math
import jax
import jax.numpy as jnp

TILE = 64
NC = 2048
NP = 2048


def with_ends(entries, key, least, high):
    shape = entries.shape
    place = [jax.random.randint(jax.random.fold_in(key, axis), (), 0, shape[axis]) for axis in range(len(shape))]
    entries = entries.at[tuple(place)].set(least)
    longest = shape.index(max(shape))
    place[longest] = (place[longest] + 1) % shape[longest]
    return entries.at[tuple(place)].set(high)


def shard_levels(rng, dims, pieces, low, high):
    loudness, own = 1.0, jax.random.fold_in(rng, 6)
    for dim, shards_of in pieces:
        draws = jnp.exp(jax.random.uniform(jax.random.fold_in(own, dim), (shards_of,), jnp.float32, low / len(pieces), high / len(pieces)))
        loudness = loudness * jnp.repeat(draws, dims[dim] // shards_of).reshape([-1 if axis == dim else 1 for axis in range(len(dims))])
    return loudness


def centred(key, extent, width, reach, shards=(), kind=jnp.bfloat16):
    values = width * jax.random.normal(key, extent, jnp.float32)
    if shards:
        values = values * shard_levels(key, extent, shards, -0.22, 0.18)
    return jnp.clip(values, -reach, reach).astype(kind)


def setup_inputs(seed: int = 0) -> dict:
    keys = jax.random.split(jax.random.key(seed), 7)
    integrals = centred(keys[0], (NC, NC), (NC // 2) ** -0.5, 0.1875, ((0, 4), (1, 8)))
    int_mask = with_ends((jax.random.randint(keys[1], (NC // TILE, NC // TILE), 0, 2) < 1).astype(jnp.int32), jax.random.fold_in(keys[1], 1), 0, 1)
    amplitudes = centred(keys[2], (NC, NP), 1.0, 6.0, ((0, 4), (1, 8)))
    domain_mask = with_ends((jax.random.randint(keys[3], (NC // TILE, NP), 0, 4) < 3).astype(jnp.int32), jax.random.fold_in(keys[3], 1), 0, 1)
    virt_energy = jnp.clip(jnp.exp(math.log(4.0) - 2.0794415 * jax.random.uniform(keys[4], (NC,), jnp.float32) ** shard_levels(keys[4], (NC,), ((0, 4),), -0.2, 0.2)), 0.5, 4.0)
    occ_energy = jnp.clip(-3.0 + 2.5 * jax.random.uniform(keys[5], (NP,), jnp.float32) ** shard_levels(keys[5], (NP,), ((0, 8),), -0.2, 0.2), -3.0, -0.5)
    return dict(integrals=integrals, int_mask=int_mask, amplitudes=amplitudes, domain_mask=domain_mask, virt_energy=virt_energy, occ_energy=occ_energy)


def reference(integrals, int_mask, amplitudes, domain_mask, virt_energy, occ_energy):
    count_rows = integrals.shape[0] // TILE
    count_cols = integrals.shape[1] // TILE
    masked_ints = (integrals.reshape(count_rows, TILE, count_cols, TILE)
                   * int_mask[:, None, :, None].astype(integrals.dtype)).reshape(integrals.shape)
    pairs = amplitudes.shape[1]
    row_mask = domain_mask[:, None, :].astype(amplitudes.dtype)
    masked_amps = (amplitudes.reshape(count_rows, TILE, pairs) * row_mask).reshape(amplitudes.shape)
    ladder = jnp.dot(masked_ints, masked_amps, preferred_element_type=jnp.float32)
    denominator = virt_energy[:, None] - occ_energy[None, :]
    scaled = ladder / denominator
    out_mask = domain_mask[:, None, :].astype(jnp.float32)
    return (scaled.reshape(count_rows, TILE, pairs) * out_mask).reshape(scaled.shape)
```

```python
import functools

import jax
import jax.numpy as jnp
from jax import lax
from jax.experimental import pallas as pl
from jax.experimental.pallas import tpu as pltpu
from jax.sharding import PartitionSpec as P

TILE = 64
MESH = pl.DeviceIdType.MESH


def flipped(index, distance, count):
    out, bit = 0, 1
    while bit < count:
        have = lax.rem(index // bit, 2)
        out = out + bit * (1 - have if (distance // bit) % 2 else have)
        bit *= 2
    return out


def kernel(R, C, a_hbm, im_ref, b_hbm, dm_ref, v_ref, o_ref, out_ref,
           a_all, b_all, acc, inv, load_sem, a_send, a_recv, sib_send, sib_recv,
           dn_send, dn_recv, up_send, up_recv):
    r, c, p = lax.axis_index("row"), lax.axis_index("col"), lax.axis_index("pair")
    q = 1 - p
    rows, width = a_hbm.shape
    depth, cols = b_hbm.shape
    parts = depth // width
    tiles = depth // TILE

    load_b = pltpu.make_async_copy(b_hbm, b_all.at[r], load_sem.at[0])
    load_a = pltpu.make_async_copy(a_hbm, a_all.at[c * 2 + p], load_sem.at[1])
    load_b.start()
    load_a.start()

    others = [flipped(c, d, C) for d in range(C)]
    barrier = pltpu.get_barrier_semaphore()

    def greet(device):
        pl.semaphore_signal(barrier, inc=1, device_id=device, device_id_type=MESH)

    greet((r, c, q))
    for d in range(1, C):
        greet((r, others[d], p))

    @pl.when(r > 0)
    def _():
        greet((r - 1, c, p))

    @pl.when(r < R - 1)
    def _():
        greet((r + 1, c, p))

    def part(block, j):
        return b_all.at[block, pl.ds(j * width, width)]

    def down(block, s, j):
        return pltpu.make_async_remote_copy(
            src_ref=part(block, j), dst_ref=part(block, j),
            send_sem=dn_send.at[s, j], recv_sem=dn_recv.at[s, j],
            device_id=(r - 1, c, p), device_id_type=MESH)

    def up(block, s, j):
        return pltpu.make_async_remote_copy(
            src_ref=part(block, j), dst_ref=part(block, j),
            send_sem=up_send.at[s, j], recv_sem=up_recv.at[s, j],
            device_id=(r + 1, c, p), device_id_type=MESH)

    def across(d):
        slot = a_all.at[c * 2 + p]
        return pltpu.make_async_remote_copy(
            src_ref=slot, dst_ref=slot, send_sem=a_send.at[d], recv_sem=a_recv.at[d],
            device_id=(r, others[d], p), device_id_type=MESH)

    def sibling(d):
        slot = a_all.at[others[d] * 2 + p]
        return pltpu.make_async_remote_copy(
            src_ref=slot, dst_ref=slot, send_sem=sib_send.at[d], recv_sem=sib_recv.at[d],
            device_id=(r, c, q), device_id_type=MESH)

    load_b.wait()
    for t in range(tiles):
        keep = dm_ref[t:t + 1, :].astype(jnp.bfloat16)
        here = pl.ds(t * TILE, TILE)
        b_all[r, here, :] = b_all[r, here, :] * keep

    pl.semaphore_wait(barrier, C + (r + R - 1) // R + (2 * R - 2 - r) // R)

    for j in range(parts):
        @pl.when(r > 0)
        def _():
            down(r, 0, j).start()

        @pl.when(r < R - 1)
        def _():
            up(r, 0, j).start()

    load_a.wait()
    lane = lax.broadcasted_iota(jnp.int32, (rows // TILE, width), 1) // TILE
    wide = jnp.zeros((rows // TILE, width), jnp.int32)
    for t in range(width // TILE):
        wide = jnp.where(lane == t, im_ref[:, t:t + 1], wide)
    wide = wide.astype(jnp.float32)
    me = c * 2 + p
    for t in range(rows // TILE):
        here = pl.ds(t * TILE, TILE)
        a_all[me, here, :] = a_all[me, here, :] * wide[t:t + 1, :].astype(jnp.bfloat16)

    for d in range(1, C):
        across(d).start()
    sibling(0).start()

    for t in range(rows // 128):
        v = jnp.broadcast_to(v_ref[:, t * 128:(t + 1) * 128], (128, 128)).T
        for u in range(cols // 128):
            lanes = slice(u * 128, (u + 1) * 128)
            factor = 1.0 / (v - o_ref[:, lanes])
            for w in range(128 // TILE):
                row = t * (128 // TILE) + w
                keep = dm_ref[row:row + 1, lanes].astype(jnp.float32)
                inv[pl.ds(row * TILE, TILE), lanes] = factor[w * TILE:(w + 1) * TILE] * keep

    def receive(s, j):
        above, below = r + s + 1, r - s - 1

        @pl.when(above < R)
        def _():
            down(above, s, j).wait_recv()

            @pl.when(r > 0)
            def _():
                down(above, s + 1, j).start()

        @pl.when(below >= 0)
        def _():
            up(below, s, j).wait_recv()

            @pl.when(r < R - 1)
            def _():
                up(below, s + 1, j).start()

    def product(block, j):
        return jnp.dot(a_all[block * parts + j], b_all[block, j * width:(j + 1) * width],
                       preferred_element_type=jnp.float32)

    def add(block, j):
        acc[...] += product(block, j)

    for j in range(parts):
        receive(0, j)
    for d in range(1, C):
        across(d).wait_recv()
        sibling(d).start()
    for d in range(C):
        pltpu.make_async_remote_copy(
            src_ref=a_all.at[others[d] * 2 + q], dst_ref=a_all.at[others[d] * 2 + q],
            send_sem=sib_send.at[d], recv_sem=sib_recv.at[d],
            device_id=(r, c, q), device_id_type=MESH).wait_recv()

    acc[...] = product(r, 0)
    for j in range(1, parts):
        add(r, j)

    for s in range(R - 1):
        for j in range(parts):
            if s > 0:
                receive(s, j)

            @pl.when(r + s + 1 < R)
            def _():
                add(r + s + 1, j)

            @pl.when(r - s - 1 >= 0)
            def _():
                add(r - s - 1, j)

    out_ref[...] = acc[...] * inv[...]

    for d in range(1, C):
        across(d).wait_send()
    for d in range(C):
        sibling(d).wait_send()
    for s in range(R - 1):
        for j in range(parts):
            @pl.when((r + s < R) & (r > 0))
            def _():
                down(r + s, s, j).wait_send()

            @pl.when((r - s >= 0) & (r < R - 1))
            def _():
                up(r - s, s, j).wait_send()


def solution(mesh):
    R, C = mesh.shape["row"], mesh.shape["col"]

    def local(integrals, int_mask, amplitudes, domain_mask, virt_energy, occ_energy):
        rows, width = integrals.shape
        depth, cols = amplitudes.shape
        parts = depth // width
        vmem = pl.BlockSpec(memory_space=pltpu.VMEM)
        hbm = pl.BlockSpec(memory_space=pl.ANY)
        dma = pltpu.SemaphoreType.DMA
        return pl.pallas_call(
            functools.partial(kernel, R, C),
            out_shape=jax.ShapeDtypeStruct((rows, cols), jnp.float32),
            in_specs=[hbm, vmem, hbm, vmem, vmem, vmem],
            out_specs=vmem,
            scratch_shapes=[
                pltpu.VMEM((C * 2, rows, width), jnp.bfloat16),
                pltpu.VMEM((R, depth, cols), jnp.bfloat16),
                pltpu.VMEM((rows, cols), jnp.float32),
                pltpu.VMEM((rows, cols), jnp.float32),
                dma((2,)), dma((C,)), dma((C,)), dma((C,)), dma((C,)),
                dma((R - 1, parts)), dma((R - 1, parts)), dma((R - 1, parts)), dma((R - 1, parts)),
            ],
            compiler_params=pltpu.CompilerParams(
                collective_id=0, has_side_effects=True, vmem_limit_bytes=48 * 2**20),
            cost_estimate=pl.CostEstimate(
                flops=2 * rows * depth * R * cols, bytes_accessed=4 * 2**20, transcendentals=0),
        )(integrals, int_mask, amplitudes, domain_mask,
          virt_energy.reshape(1, rows), occ_energy.reshape(1, cols))

    placed = (
        P("row", ("col", "pair")),
        P("row", ("col", "pair")),
        P("row", ("col", "pair")),
        P("row", ("col", "pair")),
        P("row"),
        P(("col", "pair")),
    )
    return jax.shard_map(
        local, mesh=mesh, in_specs=placed, out_specs=P("row", ("col", "pair")), check_vma=False
    )
```

```python
import functools

import jax
import jax.numpy as jnp
from jax import lax
from jax.experimental import pallas as pl
from jax.experimental.pallas import tpu as pltpu
from jax.sharding import PartitionSpec as P

TILE = 64
MESH = pl.DeviceIdType.MESH


def flipped(index, distance, count):
    out, bit = 0, 1
    while bit < count:
        have = lax.rem(index // bit, 2)
        out = out + bit * (1 - have if (distance // bit) % 2 else have)
        bit *= 2
    return out


def kernel(R, C, a_hbm, im_hbm, b_hbm, dm_hbm, v_hbm, o_hbm, out_ref,
           a_all, b_all, acc, inv, im_ref, dm_ref, v_ref, o_ref, load_sem,
           a_send, a_recv, sib_send, sib_recv, dn_send, dn_recv, up_send, up_recv):
    r, c, p = lax.axis_index("row"), lax.axis_index("col"), lax.axis_index("pair")
    q = 1 - p
    me = c * 2 + p
    rows, width = a_hbm.shape
    depth, cols = b_hbm.shape
    parts = depth // width
    half = rows // 2
    bits = [1 << i for i in range(C.bit_length() - 1)]

    loads = [
        pltpu.make_async_copy(src, dst, load_sem.at[i]) for i, (src, dst) in enumerate([
            (dm_hbm, dm_ref), (b_hbm, b_all.at[r]), (im_hbm, im_ref), (a_hbm, a_all.at[me]),
            (v_hbm, v_ref), (o_hbm, o_ref)])
    ]
    for load in loads:
        load.start()

    others = [flipped(c, d, C) for d in range(C)]
    barrier = pltpu.get_barrier_semaphore()

    def greet(device):
        pl.semaphore_signal(barrier, inc=1, device_id=device, device_id_type=MESH)

    greet((r, c, q))
    for e in bits:
        greet((r, others[e], p))

    @pl.when(r > 0)
    def _():
        greet((r - 1, c, p))

    @pl.when(r < R - 1)
    def _():
        greet((r + 1, c, p))

    def part(block, j):
        return b_all.at[block, pl.ds(j * width, width)]

    def down(block, s, j):
        return pltpu.make_async_remote_copy(
            src_ref=part(block, j), dst_ref=part(block, j),
            send_sem=dn_send.at[s, j], recv_sem=dn_recv.at[s, j],
            device_id=(r - 1, c, p), device_id_type=MESH)

    def up(block, s, j):
        return pltpu.make_async_remote_copy(
            src_ref=part(block, j), dst_ref=part(block, j),
            send_sem=up_send.at[s, j], recv_sem=up_recv.at[s, j],
            device_id=(r + 1, c, p), device_id_type=MESH)

    def across(d, e, h):
        piece = a_all.at[others[d] * 2 + p, pl.ds(h * half, half)]
        return pltpu.make_async_remote_copy(
            src_ref=piece, dst_ref=piece,
            send_sem=a_send.at[d + e, h], recv_sem=a_recv.at[d + e, h],
            device_id=(r, others[e], p), device_id_type=MESH)

    def sibling(d, h, core=None):
        piece = a_all.at[others[d] * 2 + (p if core is None else core), pl.ds(h * half, half)]
        return pltpu.make_async_remote_copy(
            src_ref=piece, dst_ref=piece,
            send_sem=sib_send.at[d, h], recv_sem=sib_recv.at[d, h],
            device_id=(r, c, q), device_id_type=MESH)

    def onward(d, h):
        if d == 0:
            return bits
        low, high = d & -d, 1 << (d.bit_length() - 1)
        return [e for e in bits if (e < low if h == 0 else e > high)]

    def arrives(d, h):
        low, high = d & -d, 1 << (d.bit_length() - 1)
        e = low if h == 0 else high
        piece = a_all.at[others[d] * 2 + p, pl.ds(h * half, half)]
        pltpu.make_async_remote_copy(
            src_ref=piece, dst_ref=piece,
            send_sem=a_send.at[d, h], recv_sem=a_recv.at[d, h],
            device_id=(r, others[e], p), device_id_type=MESH).wait_recv()
        for e in onward(d, h):
            across(d, e, h).start()
        sibling(d, h).start()

    loads[0].wait()
    loads[1].wait()
    for t in range(depth // TILE):
        keep = dm_ref[t:t + 1, :].astype(jnp.bfloat16)
        here = pl.ds(t * TILE, TILE)
        b_all[r, here, :] = b_all[r, here, :] * keep

    pl.semaphore_wait(barrier, 1 + len(bits) + (r + R - 1) // R + (2 * R - 2 - r) // R)

    for j in range(parts):
        @pl.when(r > 0)
        def _():
            down(r, 0, j).start()

        @pl.when(r < R - 1)
        def _():
            up(r, 0, j).start()

    loads[2].wait()
    loads[3].wait()
    lane = lax.broadcasted_iota(jnp.int32, (1, width), 1) // TILE
    for t in range(rows // TILE):
        keep = jnp.zeros((1, width), jnp.float32)
        for u in range(width // TILE):
            keep = jnp.where(lane == u, im_ref[u:u + 1, t:t + 1].astype(jnp.float32), keep)
        here = pl.ds(t * TILE, TILE)
        a_all[me, here, :] = a_all[me, here, :] * keep.astype(jnp.bfloat16)

    for h in (1, 0):
        for e in bits:
            g = h if 2 * e < C else 1 - h
            across(0, e, g).start()
    for h in range(2):
        sibling(0, h).start()

    loads[4].wait()
    loads[5].wait()
    for t in range(rows // 128):
        v = jnp.broadcast_to(v_ref[:, t * 128:(t + 1) * 128], (128, 128)).T
        for u in range(cols // 128):
            lanes = slice(u * 128, (u + 1) * 128)
            factor = 1.0 / (v - o_ref[:, lanes])
            for w in range(128 // TILE):
                row = t * (128 // TILE) + w
                keep = dm_ref[row:row + 1, lanes].astype(jnp.float32)
                inv[pl.ds(row * TILE, TILE), lanes] = factor[w * TILE:(w + 1) * TILE] * keep

    def receive(s, j):
        above, below = r + s + 1, r - s - 1

        @pl.when(above < R)
        def _():
            down(above, s, j).wait_recv()

            @pl.when(r > 0)
            def _():
                down(above, s + 1, j).start()

        @pl.when(below >= 0)
        def _():
            up(below, s, j).wait_recv()

            @pl.when(r < R - 1)
            def _():
                up(below, s + 1, j).start()

    def product(block, j):
        return jnp.dot(a_all[block * parts + j], b_all[block, j * width:(j + 1) * width],
                       preferred_element_type=jnp.float32)

    def add(s, j):
        @pl.when(r + s + 1 < R)
        def _():
            acc[...] += product(r + s + 1, j)

        @pl.when(r - s - 1 >= 0)
        def _():
            acc[...] += product(r - s - 1, j)

    along = [(0, j) for j in range(parts)]
    near = [d for d in range(1, C) if d in bits]
    for h in (1, 0):
        for d in near:
            arrives(d, h if 2 * d < C else 1 - h)
        if along:
            receive(*along.pop(0))
    while along:
        receive(*along.pop(0))
    for d in sorted(range(1, C), key=lambda d: d.bit_count()):
        if d not in near:
            for h in range(2):
                arrives(d, h)
    later = [(s, j) for s in range(1, R - 1) for j in range(parts)]
    if later:
        receive(*later[0])
    for d in range(C):
        for h in range(2):
            sibling(d, h, q).wait_recv()

    acc[...] = product(r, 0)
    for j in range(1, parts):
        acc[...] += product(r, j)
    due = [(0, j) for j in range(parts)]
    for item in later[:1]:
        add(*due.pop(0))
        due.append(item)
    for item in later[1:]:
        if item == later[-1]:
            while due:
                add(*due.pop(0))
        receive(*item)
        due.append(item)
        if item != later[-1]:
            add(*due.pop(0))
    while due:
        add(*due.pop(0))

    out_ref[...] = acc[...] * inv[...]

    for d in range(C):
        for h in range(2):
            sibling(d, h).wait_send()
            for e in onward(d, h):
                across(d, e, h).wait_send()
    for s in range(R - 1):
        for j in range(parts):
            @pl.when((r + s < R) & (r > 0))
            def _():
                down(r + s, s, j).wait_send()

            @pl.when((r - s >= 0) & (r < R - 1))
            def _():
                up(r - s, s, j).wait_send()


def solution(mesh):
    R, C = mesh.shape["row"], mesh.shape["col"]

    def local(integrals, int_mask, amplitudes, domain_mask, virt_energy, occ_energy):
        rows, width = integrals.shape
        depth, cols = amplitudes.shape
        parts = depth // width
        vmem = pl.BlockSpec(memory_space=pltpu.VMEM)
        hbm = pl.BlockSpec(memory_space=pltpu.HBM)
        dma = pltpu.SemaphoreType.DMA
        return pl.pallas_call(
            functools.partial(kernel, R, C),
            out_shape=jax.ShapeDtypeStruct((rows, cols), jnp.float32),
            in_specs=[hbm] * 6,
            out_specs=vmem,
            scratch_shapes=[
                pltpu.VMEM((C * 2, rows, width), jnp.bfloat16),
                pltpu.VMEM((R, depth, cols), jnp.bfloat16),
                pltpu.VMEM((rows, cols), jnp.float32),
                pltpu.VMEM((rows, cols), jnp.float32),
                pltpu.VMEM(int_mask.shape[::-1], jnp.int32),
                pltpu.VMEM(domain_mask.shape, jnp.int32),
                pltpu.VMEM((1, rows), jnp.float32),
                pltpu.VMEM((1, cols), jnp.float32),
                dma((6,)), dma((C, 2)), dma((C, 2)), dma((C, 2)), dma((C, 2)),
                dma((R - 1, parts)), dma((R - 1, parts)), dma((R - 1, parts)), dma((R - 1, parts)),
            ],
            compiler_params=pltpu.CompilerParams(
                collective_id=0, has_side_effects=True, vmem_limit_bytes=48 * 2**20),
            cost_estimate=pl.CostEstimate(
                flops=2 * rows * depth * R * cols, bytes_accessed=4 * 2**20, transcendentals=0),
        )(integrals, int_mask.T, amplitudes, domain_mask,
          virt_energy.reshape(1, rows), occ_energy.reshape(1, cols))

    placed = (
        P("row", ("col", "pair")),
        P("row", ("col", "pair")),
        P("row", ("col", "pair")),
        P("row", ("col", "pair")),
        P("row"),
        P(("col", "pair")),
    )
    return jax.shard_map(
        local, mesh=mesh, in_specs=placed, out_specs=P("row", ("col", "pair")), check_vma=False
    )
```

```python
import functools

import jax
import jax.numpy as jnp
from jax import lax
from jax.experimental import pallas as pl
from jax.experimental.pallas import tpu as pltpu
from jax.sharding import PartitionSpec as P

TILE = 64
PIECES = 4
MESH = pl.DeviceIdType.MESH


def flipped(index, distance, count):
    out, bit = 0, 1
    while bit < count:
        have = lax.rem(index // bit, 2)
        out = out + bit * (1 - have if (distance // bit) % 2 else have)
        bit *= 2
    return out


def kernel(R, C, a_hbm, im_hbm, b_hbm, dm_hbm, v_hbm, o_hbm, out_ref,
           a_all, b_all, acc, inv, im_ref, dm_ref, v_ref, o_ref, load_sem, store_sem,
           a_send, a_recv, sib_send, sib_recv, dn_send, dn_recv, up_send, up_recv):
    r, c, p = lax.axis_index("row"), lax.axis_index("col"), lax.axis_index("pair")
    q = 1 - p
    me = c * 2 + p
    rows, width = a_hbm.shape
    depth, cols = b_hbm.shape
    parts = depth // width
    half = rows // 2
    bits = [1 << i for i in range(C.bit_length() - 1)]

    loads = [
        pltpu.make_async_copy(src, dst, load_sem.at[i]) for i, (src, dst) in enumerate([
            (dm_hbm, dm_ref), (b_hbm, b_all.at[r]), (im_hbm, im_ref), (a_hbm, a_all.at[me]),
            (v_hbm, v_ref), (o_hbm, o_ref)])
    ]
    for load in loads:
        load.start()

    others = [flipped(c, d, C) for d in range(C)]
    barrier = pltpu.get_barrier_semaphore()

    def greet(device):
        pl.semaphore_signal(barrier, inc=1, device_id=device, device_id_type=MESH)

    greet((r, c, q))
    for e in bits:
        greet((r, others[e], p))

    @pl.when(r > 0)
    def _():
        greet((r - 1, c, p))

    @pl.when(r < R - 1)
    def _():
        greet((r + 1, c, p))

    def part(block, j):
        return b_all.at[block, pl.ds(j * width, width)]

    def down(block, s, j):
        return pltpu.make_async_remote_copy(
            src_ref=part(block, j), dst_ref=part(block, j),
            send_sem=dn_send.at[s, j], recv_sem=dn_recv.at[s, j],
            device_id=(r - 1, c, p), device_id_type=MESH)

    def up(block, s, j):
        return pltpu.make_async_remote_copy(
            src_ref=part(block, j), dst_ref=part(block, j),
            send_sem=up_send.at[s, j], recv_sem=up_recv.at[s, j],
            device_id=(r + 1, c, p), device_id_type=MESH)

    def across(d, e, h):
        piece = a_all.at[others[d] * 2 + p, pl.ds(h * half, half)]
        return pltpu.make_async_remote_copy(
            src_ref=piece, dst_ref=piece,
            send_sem=a_send.at[d + e, h], recv_sem=a_recv.at[d + e, h],
            device_id=(r, others[e], p), device_id_type=MESH)

    def sibling(d, h, core=None):
        piece = a_all.at[others[d] * 2 + (p if core is None else core), pl.ds(h * half, half)]
        return pltpu.make_async_remote_copy(
            src_ref=piece, dst_ref=piece,
            send_sem=sib_send.at[d, h], recv_sem=sib_recv.at[d, h],
            device_id=(r, c, q), device_id_type=MESH)

    def onward(d, h):
        if d == 0:
            return bits
        low, high = d & -d, 1 << (d.bit_length() - 1)
        return [e for e in bits if (e < low if h == 0 else e > high)]

    def arrives(d, h):
        low, high = d & -d, 1 << (d.bit_length() - 1)
        e = low if h == 0 else high
        piece = a_all.at[others[d] * 2 + p, pl.ds(h * half, half)]
        pltpu.make_async_remote_copy(
            src_ref=piece, dst_ref=piece,
            send_sem=a_send.at[d, h], recv_sem=a_recv.at[d, h],
            device_id=(r, others[e], p), device_id_type=MESH).wait_recv()
        for e in onward(d, h):
            across(d, e, h).start()
        sibling(d, h).start()

    loads[0].wait()
    loads[1].wait()
    for t in range(depth // TILE):
        keep = dm_ref[t:t + 1, :].astype(jnp.bfloat16)
        here = pl.ds(t * TILE, TILE)
        b_all[r, here, :] = b_all[r, here, :] * keep

    pl.semaphore_wait(barrier, 1 + len(bits) + (r + R - 1) // R + (2 * R - 2 - r) // R)

    for j in range(parts):
        @pl.when(r > 0)
        def _():
            down(r, 0, j).start()

        @pl.when(r < R - 1)
        def _():
            up(r, 0, j).start()

    loads[2].wait()
    loads[3].wait()
    lane = lax.broadcasted_iota(jnp.int32, (1, width), 1) // TILE
    for t in range(rows // TILE):
        keep = jnp.zeros((1, width), jnp.float32)
        for u in range(width // TILE):
            keep = jnp.where(lane == u, im_ref[u:u + 1, t:t + 1].astype(jnp.float32), keep)
        here = pl.ds(t * TILE, TILE)
        a_all[me, here, :] = a_all[me, here, :] * keep.astype(jnp.bfloat16)

    for h in (1, 0):
        for e in bits:
            g = h if 2 * e < C else 1 - h
            across(0, e, g).start()
    for h in range(2):
        sibling(0, h).start()

    loads[4].wait()
    loads[5].wait()
    for t in range(rows // 128):
        v = jnp.broadcast_to(v_ref[:, t * 128:(t + 1) * 128], (128, 128)).T
        for u in range(cols // 128):
            lanes = slice(u * 128, (u + 1) * 128)
            factor = 1.0 / (v - o_ref[:, lanes])
            for w in range(128 // TILE):
                row = t * (128 // TILE) + w
                keep = dm_ref[row:row + 1, lanes].astype(jnp.float32)
                inv[pl.ds(row * TILE, TILE), lanes] = factor[w * TILE:(w + 1) * TILE] * keep

    def receive(s, j):
        above, below = r + s + 1, r - s - 1

        @pl.when(above < R)
        def _():
            down(above, s, j).wait_recv()

            @pl.when(r > 0)
            def _():
                down(above, s + 1, j).start()

        @pl.when(below >= 0)
        def _():
            up(below, s, j).wait_recv()

            @pl.when(r < R - 1)
            def _():
                up(below, s + 1, j).start()

    whole = pl.ds(0, rows)

    def product(block, j, here=whole):
        return jnp.dot(a_all[block * parts + j, here, :], b_all[block, j * width:(j + 1) * width],
                       preferred_element_type=jnp.float32)

    def add(s, j, here=whole):
        @pl.when(r + s + 1 < R)
        def _():
            acc[here, :] += product(r + s + 1, j, here)

        @pl.when(r - s - 1 >= 0)
        def _():
            acc[here, :] += product(r - s - 1, j, here)

    along = [(0, j) for j in range(parts)]
    near = [d for d in range(1, C) if d in bits]
    for h in (1, 0):
        for d in near:
            arrives(d, h if 2 * d < C else 1 - h)
        if along:
            receive(*along.pop(0))
    while along:
        receive(*along.pop(0))
    for d in sorted(range(1, C), key=lambda d: d.bit_count()):
        if d not in near:
            for h in range(2):
                arrives(d, h)
    later = [(s, j) for s in range(1, R - 1) for j in range(parts)]
    if later:
        receive(*later[0])
    for d in range(C):
        for h in range(2):
            sibling(d, h, q).wait_recv()

    acc[...] = product(r, 0)
    for j in range(1, parts):
        acc[...] += product(r, j)
    due = [(0, j) for j in range(parts)]
    for item in later[:1]:
        add(*due.pop(0))
        due.append(item)
    for item in later[1:]:
        if item == later[-1]:
            while due:
                add(*due.pop(0))
        receive(*item)
        due.append(item)
        if item != later[-1]:
            add(*due.pop(0))

    stores = []
    for t in range(PIECES):
        here = pl.ds(t * (rows // PIECES), rows // PIECES)
        for s, j in due:
            add(s, j, here)
        acc[here, :] = acc[here, :] * inv[here, :]
        stores.append(pltpu.make_async_copy(acc.at[here], out_ref.at[here], store_sem.at[t]))
        stores[-1].start()

    for d in range(C):
        for h in range(2):
            sibling(d, h).wait_send()
            for e in onward(d, h):
                across(d, e, h).wait_send()
    for s in range(R - 1):
        for j in range(parts):
            @pl.when((r + s < R) & (r > 0))
            def _():
                down(r + s, s, j).wait_send()

            @pl.when((r - s >= 0) & (r < R - 1))
            def _():
                up(r - s, s, j).wait_send()
    for store in stores:
        store.wait()


def solution(mesh):
    R, C = mesh.shape["row"], mesh.shape["col"]

    def local(integrals, int_mask, amplitudes, domain_mask, virt_energy, occ_energy):
        rows, width = integrals.shape
        depth, cols = amplitudes.shape
        parts = depth // width
        hbm = pl.BlockSpec(memory_space=pl.ANY)
        dma = pltpu.SemaphoreType.DMA
        return pl.pallas_call(
            functools.partial(kernel, R, C),
            out_shape=jax.ShapeDtypeStruct((rows, cols), jnp.float32),
            in_specs=[hbm] * 6,
            out_specs=hbm,
            scratch_shapes=[
                pltpu.VMEM((C * 2, rows, width), jnp.bfloat16),
                pltpu.VMEM((R, depth, cols), jnp.bfloat16),
                pltpu.VMEM((rows, cols), jnp.float32),
                pltpu.VMEM((rows, cols), jnp.float32),
                pltpu.VMEM(int_mask.shape[::-1], jnp.int32),
                pltpu.VMEM(domain_mask.shape, jnp.int32),
                pltpu.VMEM((1, rows), jnp.float32),
                pltpu.VMEM((1, cols), jnp.float32),
                dma((6,)), dma((PIECES,)), dma((C, 2)), dma((C, 2)), dma((C, 2)), dma((C, 2)),
                dma((R - 1, parts)), dma((R - 1, parts)), dma((R - 1, parts)), dma((R - 1, parts)),
            ],
            compiler_params=pltpu.CompilerParams(
                collective_id=0, has_side_effects=True, vmem_limit_bytes=62 * 2**20),
            cost_estimate=pl.CostEstimate(
                flops=2 * rows * depth * R * cols, bytes_accessed=4 * 2**20, transcendentals=0),
        )(integrals, int_mask.T, amplitudes, domain_mask,
          virt_energy.reshape(1, rows), occ_energy.reshape(1, cols))

    placed = (
        P("row", ("col", "pair")),
        P("row", ("col", "pair")),
        P("row", ("col", "pair")),
        P("row", ("col", "pair")),
        P("row"),
        P(("col", "pair")),
    )
    return jax.shard_map(
        local, mesh=mesh, in_specs=placed, out_specs=P("row", ("col", "pair")), check_vma=False
    )
```

```python
import functools

import jax
import jax.numpy as jnp
from jax import lax
from jax.experimental import pallas as pl
from jax.experimental.pallas import tpu as pltpu
from jax.sharding import PartitionSpec as P

TILE = 64
PIECES = 1
MESH = pl.DeviceIdType.MESH


def flipped(index, distance, count):
    out, bit = 0, 1
    while bit < count:
        have = lax.rem(index // bit, 2)
        out = out + bit * (1 - have if (distance // bit) % 2 else have)
        bit *= 2
    return out


def kernel(R, C, a_hbm, im_hbm, b_hbm, dm_hbm, v_hbm, o_hbm, out_ref,
           a_all, b_all, acc, inv, im_ref, dm_ref, v_ref, o_ref, load_sem, store_sem,
           a_send, a_recv, sib_send, sib_recv, dn_send, dn_recv, up_send, up_recv):
    r, c, p = lax.axis_index("row"), lax.axis_index("col"), lax.axis_index("pair")
    q = 1 - p
    me = c * 2 + p
    rows, width = a_hbm.shape
    depth, cols = b_hbm.shape
    parts = depth // width
    half = rows // 2
    bits = [1 << i for i in range(C.bit_length() - 1)]

    loads = [
        pltpu.make_async_copy(src, dst, load_sem.at[i]) for i, (src, dst) in enumerate([
            (dm_hbm, dm_ref), (b_hbm, b_all.at[r]), (im_hbm, im_ref), (a_hbm, a_all.at[me]),
            (v_hbm, v_ref), (o_hbm, o_ref)])
    ]
    for load in loads:
        load.start()

    others = [flipped(c, d, C) for d in range(C)]
    barrier = pltpu.get_barrier_semaphore()

    def greet(device):
        pl.semaphore_signal(barrier, inc=1, device_id=device, device_id_type=MESH)

    greet((r, c, q))
    for e in bits:
        greet((r, others[e], p))

    @pl.when(r > 0)
    def _():
        greet((r - 1, c, p))

    @pl.when(r < R - 1)
    def _():
        greet((r + 1, c, p))

    def part(block, j):
        return b_all.at[block, pl.ds(j * width, width)]

    def down(block, s, j):
        return pltpu.make_async_remote_copy(
            src_ref=part(block, j), dst_ref=part(block, j),
            send_sem=dn_send.at[s, j], recv_sem=dn_recv.at[s, j],
            device_id=(r - 1, c, p), device_id_type=MESH)

    def up(block, s, j):
        return pltpu.make_async_remote_copy(
            src_ref=part(block, j), dst_ref=part(block, j),
            send_sem=up_send.at[s, j], recv_sem=up_recv.at[s, j],
            device_id=(r + 1, c, p), device_id_type=MESH)

    def across(d, e, h):
        piece = a_all.at[others[d] * 2 + p, pl.ds(h * half, half)]
        return pltpu.make_async_remote_copy(
            src_ref=piece, dst_ref=piece,
            send_sem=a_send.at[d + e, h], recv_sem=a_recv.at[d + e, h],
            device_id=(r, others[e], p), device_id_type=MESH)

    def sibling(d, h, core=None):
        piece = a_all.at[others[d] * 2 + (p if core is None else core), pl.ds(h * half, half)]
        return pltpu.make_async_remote_copy(
            src_ref=piece, dst_ref=piece,
            send_sem=sib_send.at[d, h], recv_sem=sib_recv.at[d, h],
            device_id=(r, c, q), device_id_type=MESH)

    def onward(d, h):
        if d == 0:
            return bits
        low, high = d & -d, 1 << (d.bit_length() - 1)
        return [e for e in bits if (e < low if h == 0 else e > high)]

    def arrives(d, h):
        low, high = d & -d, 1 << (d.bit_length() - 1)
        e = low if h == 0 else high
        piece = a_all.at[others[d] * 2 + p, pl.ds(h * half, half)]
        pltpu.make_async_remote_copy(
            src_ref=piece, dst_ref=piece,
            send_sem=a_send.at[d, h], recv_sem=a_recv.at[d, h],
            device_id=(r, others[e], p), device_id_type=MESH).wait_recv()
        for e in onward(d, h):
            across(d, e, h).start()
        sibling(d, h).start()

    loads[0].wait()
    loads[1].wait()
    for t in range(depth // TILE):
        keep = dm_ref[t:t + 1, :].astype(jnp.bfloat16)
        here = pl.ds(t * TILE, TILE)
        b_all[r, here, :] = b_all[r, here, :] * keep

    pl.semaphore_wait(barrier, 1 + len(bits) + (r + R - 1) // R + (2 * R - 2 - r) // R)

    for j in range(parts):
        @pl.when(r > 0)
        def _():
            down(r, 0, j).start()

        @pl.when(r < R - 1)
        def _():
            up(r, 0, j).start()

    loads[2].wait()
    loads[3].wait()
    lane = lax.broadcasted_iota(jnp.int32, (1, width), 1) // TILE
    for t in range(rows // TILE):
        keep = jnp.zeros((1, width), jnp.float32)
        for u in range(width // TILE):
            keep = jnp.where(lane == u, im_ref[u:u + 1, t:t + 1].astype(jnp.float32), keep)
        here = pl.ds(t * TILE, TILE)
        a_all[me, here, :] = a_all[me, here, :] * keep.astype(jnp.bfloat16)

    for h in (1, 0):
        for e in bits:
            g = h if 2 * e < C else 1 - h
            across(0, e, g).start()
    for h in range(2):
        sibling(0, h).start()

    loads[4].wait()
    loads[5].wait()
    for t in range(rows // 128):
        v = jnp.broadcast_to(v_ref[:, t * 128:(t + 1) * 128], (128, 128)).T
        for u in range(cols // 128):
            lanes = slice(u * 128, (u + 1) * 128)
            factor = 1.0 / (v - o_ref[:, lanes])
            for w in range(128 // TILE):
                row = t * (128 // TILE) + w
                keep = dm_ref[row:row + 1, lanes].astype(jnp.float32)
                inv[pl.ds(row * TILE, TILE), lanes] = factor[w * TILE:(w + 1) * TILE] * keep

    def receive(s, j):
        above, below = r + s + 1, r - s - 1

        @pl.when(above < R)
        def _():
            down(above, s, j).wait_recv()

            @pl.when(r > 0)
            def _():
                down(above, s + 1, j).start()

        @pl.when(below >= 0)
        def _():
            up(below, s, j).wait_recv()

            @pl.when(r < R - 1)
            def _():
                up(below, s + 1, j).start()

    whole = pl.ds(0, rows)

    def product(block, j, here=whole):
        return jnp.dot(a_all[block * parts + j, here, :], b_all[block, j * width:(j + 1) * width],
                       preferred_element_type=jnp.float32)

    def add(s, j, here=whole):
        @pl.when(r + s + 1 < R)
        def _():
            acc[here, :] += product(r + s + 1, j, here)

        @pl.when(r - s - 1 >= 0)
        def _():
            acc[here, :] += product(r - s - 1, j, here)

    along = [(0, j) for j in range(parts)]
    near = [d for d in range(1, C) if d in bits]
    for h in (1, 0):
        for d in near:
            arrives(d, h if 2 * d < C else 1 - h)
        if along:
            receive(*along.pop(0))
    while along:
        receive(*along.pop(0))
    for d in sorted(range(1, C), key=lambda d: d.bit_count()):
        if d not in near:
            for h in range(2):
                arrives(d, h)
    later = [(s, j) for s in range(1, R - 1) for j in range(parts)]
    if later:
        receive(*later[0])
    for d in range(C):
        for h in range(2):
            sibling(d, h, q).wait_recv()

    acc[...] = product(r, 0)
    for j in range(1, parts):
        acc[...] += product(r, j)
    due = [(0, j) for j in range(parts)]
    for item in later[:1]:
        add(*due.pop(0))
        due.append(item)
    for item in later[1:]:
        if item == later[-1]:
            while due:
                add(*due.pop(0))
        receive(*item)
        due.append(item)
        if item != later[-1]:
            add(*due.pop(0))

    stores = []
    for t in range(PIECES):
        here = pl.ds(t * (rows // PIECES), rows // PIECES)
        for s, j in due:
            add(s, j, here)
        acc[here, :] = acc[here, :] * inv[here, :]
        stores.append(pltpu.make_async_copy(acc.at[here], out_ref.at[here], store_sem.at[t]))
        stores[-1].start()

    for d in range(C):
        for h in range(2):
            sibling(d, h).wait_send()
            for e in onward(d, h):
                across(d, e, h).wait_send()
    for s in range(R - 1):
        for j in range(parts):
            @pl.when((r + s < R) & (r > 0))
            def _():
                down(r + s, s, j).wait_send()

            @pl.when((r - s >= 0) & (r < R - 1))
            def _():
                up(r - s, s, j).wait_send()
    for store in stores:
        store.wait()


def solution(mesh):
    R, C = mesh.shape["row"], mesh.shape["col"]

    def local(integrals, int_mask, amplitudes, domain_mask, virt_energy, occ_energy):
        rows, width = integrals.shape
        depth, cols = amplitudes.shape
        parts = depth // width
        hbm = pl.BlockSpec(memory_space=pl.ANY)
        dma = pltpu.SemaphoreType.DMA
        return pl.pallas_call(
            functools.partial(kernel, R, C),
            out_shape=jax.ShapeDtypeStruct((rows, cols), jnp.float32),
            in_specs=[hbm] * 6,
            out_specs=hbm,
            scratch_shapes=[
                pltpu.VMEM((C * 2, rows, width), jnp.bfloat16),
                pltpu.VMEM((R, depth, cols), jnp.bfloat16),
                pltpu.VMEM((rows, cols), jnp.float32),
                pltpu.VMEM((rows, cols), jnp.float32),
                pltpu.VMEM(int_mask.shape[::-1], jnp.int32),
                pltpu.VMEM(domain_mask.shape, jnp.int32),
                pltpu.VMEM((1, rows), jnp.float32),
                pltpu.VMEM((1, cols), jnp.float32),
                dma((6,)), dma((PIECES,)), dma((C, 2)), dma((C, 2)), dma((C, 2)), dma((C, 2)),
                dma((R - 1, parts)), dma((R - 1, parts)), dma((R - 1, parts)), dma((R - 1, parts)),
            ],
            compiler_params=pltpu.CompilerParams(
                collective_id=0, has_side_effects=True, vmem_limit_bytes=62 * 2**20),
            cost_estimate=pl.CostEstimate(
                flops=2 * rows * depth * R * cols, bytes_accessed=4 * 2**20, transcendentals=0),
        )(integrals, int_mask.T, amplitudes, domain_mask,
          virt_energy.reshape(1, rows), occ_energy.reshape(1, cols))

    placed = (
        P("row", ("col", "pair")),
        P("row", ("col", "pair")),
        P("row", ("col", "pair")),
        P("row", ("col", "pair")),
        P("row"),
        P(("col", "pair")),
    )
    return jax.shard_map(
        local, mesh=mesh, in_specs=placed, out_specs=P("row", ("col", "pair")), check_vma=False
    )
```
